256 devices in a mesh: ctx: 32 (over z_hi, x, y), tp: 8 (over z_lo, core).
Axes of the slice: x: 4, y: 4, z: 8 (z_hi: 2, z_lo: 4; z = z_hi * 4 + z_lo), core: 2. Of those that a mesh axis runs over, the one named last changes fastest.
Arguments:
- hidden: bfloat16 [16384, 4096], P('ctx', 'tp'), may hold values from -6 to 6
- norm_gain: float32 [4096], replicated, may hold values from 0.5 to 10
- w_query: bfloat16 [4096, 4096], P('ctx', 'tp'), may hold values from -0.09375 to 0.09375
- w_key: bfloat16 [4096, 512], P('ctx'), may hold values from -0.09375 to 0.09375
- w_value: bfloat16 [4096, 512], P('ctx'), may hold values from -0.09375 to 0.09375
- w_out: bfloat16 [4096, 4096], P('tp', 'ctx'), may hold values from -0.09375 to 0.09375
- kept_rows: int32 [32, 320], replicated, may hold values from 0 to 511, as said below
- kept_count: int32 [32], replicated, may hold values from 192 to 320, as said below
Outputs:
- layer_out: bfloat16 [16384, 4096], P('ctx', 'tp')
The draws below stay inside these ranges and needn't reach their ends.
Inputs may be any that keep to these rules, and one draw needn't show every extreme that they name: `kept_rows`: each row is sorted; its first kept_count entries are distinct and increasing, and the entries after them repeat the last kept one. `kept_count`: some shard keeps exactly 320 positions.
All inputs are finite; a program needn't handle non-finite values.
Results may differ from the reference program's by a relative error of at most 0.019.
The reference program's roundings to bfloat16 on the way (of `rows`, `normed`, `values` and `attended`) count: a program that leaves them out, or rounds other values in their place, can miss the bound.
Values may be sent and summed in bfloat16 or wider, within the bound.
No kernel may reach another device: no remote copies, remote signals or barrier semaphores. Data moves between devices by JAX's collectives and lax.ppermute only.
A program may use at most 64 MiB of HBM per device.

```python
import math
import jax
import jax.numpy as jnp
from jax import lax

WIDTH = 4096
Q_HEADS = 32
KV_HEADS = 4
HEAD_DIM = 128
TOK_DEV = 512
CAP = 320
SHARDS = 32
SEQ = 16384


def kept_lists(key):
    first_key, second_key, third_key = jax.random.split(key, 3)
    counts = jax.random.randint(first_key, (SHARDS,), 3 * TOK_DEV // 8, CAP + 1, dtype=jnp.int32)
    fullest = jax.random.randint(second_key, (), 0, SHARDS, dtype=jnp.int32)
    counts = jnp.where(jnp.arange(SHARDS, dtype=jnp.int32) == fullest, CAP, counts)
    shard_keys = jax.random.split(third_key, SHARDS)
    shuffled = jax.vmap(lambda shard_key: jax.random.permutation(shard_key, TOK_DEV))(shard_keys)
    shuffled = shuffled[:, :CAP].astype(jnp.int32)
    live_slot = jnp.arange(CAP, dtype=jnp.int32)[None, :] < counts[:, None]
    ordered = jnp.sort(jnp.where(live_slot, shuffled, TOK_DEV), axis=1)
    last_kept = jnp.take_along_axis(ordered, (counts - 1)[:, None], axis=1)
    return (jnp.where(live_slot, ordered, last_kept).astype(jnp.int32), counts.astype(jnp.int32))


def draw_kept_rows(key, part):
    return kept_lists(key)[0]


def draw_kept_count(key, part):
    return kept_lists(key)[1]


def draw_norm_gain(key, part):
    key = jax.random.fold_in(key, 7)
    return jax.random.uniform(key, (WIDTH,), jnp.float32, 0.5, 1.5)


def block_levels(key, dims, cuts, least, largest):
    factor_of = 1.0
    for position, parts in cuts:
        steps = jax.random.uniform(jax.random.fold_in(jax.random.fold_in(key, 6), position), (parts,), jnp.float32, least / len(cuts), largest / len(cuts))
        factor_of = factor_of * jnp.repeat(jnp.exp(steps), dims[position] // parts).reshape((-1,) + (1,) * (len(dims) - 1 - position))
    return factor_of


def noise(key, dims, scale, reach, pieces=(), held_as=jnp.bfloat16):
    drawn = scale * jax.random.normal(key, dims, jnp.float32)
    if pieces:
        drawn = drawn * block_levels(key, dims, pieces, -0.22, 0.18)
    return jnp.clip(drawn, -reach, reach).astype(held_as)


def setup_inputs(seed: int = 0) -> dict:
    key_of = jax.random.split(jax.random.key(seed), 9)
    hidden = noise(key_of[0], (SEQ, WIDTH), 1.0, 6.0, ((0, 32), (1, 8)))
    norm_gain = draw_norm_gain(jax.random.fold_in(key_of[8], 71), 0)
    w_query = noise(key_of[2], (WIDTH, Q_HEADS * HEAD_DIM), WIDTH ** -0.5, 0.09375, ((0, 32), (1, 8)))
    w_key = noise(key_of[3], (WIDTH, KV_HEADS * HEAD_DIM), WIDTH ** -0.5, 0.09375, ((0, 32),))
    w_value = noise(key_of[4], (WIDTH, KV_HEADS * HEAD_DIM), WIDTH ** -0.5, 0.09375, ((0, 32),))
    w_out = noise(key_of[5], (Q_HEADS * HEAD_DIM, WIDTH), (Q_HEADS * HEAD_DIM) ** -0.5, 0.09375, ((0, 8), (1, 32)))
    kept_rows = draw_kept_rows(jax.random.fold_in(key_of[8], 71), 0)
    kept_count = draw_kept_count(jax.random.fold_in(key_of[8], 71), 0)
    return dict(hidden=hidden, norm_gain=norm_gain, w_query=w_query, w_key=w_key, w_value=w_value, w_out=w_out, kept_rows=kept_rows, kept_count=kept_count)


EPSILON = 1e-05
ROPE_BASE = 10000.0

def rms_rows(rows, norm_gain):
    values = rows.astype(jnp.float32)
    spread = lax.optimization_barrier(jnp.mean(values * values, axis=-1, keepdims=True))
    return (values * lax.rsqrt(spread + EPSILON) * norm_gain).astype(jnp.bfloat16)

def rotary(vectors, positions):
    head_width = vectors.shape[-1]
    halfway = head_width // 2
    exponent = jnp.arange(halfway, dtype=jnp.float32) * (2.0 / head_width)
    inverse = jnp.exp(-math.log(ROPE_BASE) * exponent)
    angles = positions.astype(jnp.float32)[:, None] * inverse[None, :]
    cosine = jnp.cos(angles)[:, None, :]
    sine_part = jnp.sin(angles)[:, None, :]
    first_half = vectors[..., :halfway]
    second = vectors[..., halfway:]
    return jnp.concatenate([first_half * cosine - second * sine_part, second * cosine + first_half * sine_part], axis=-1)

def reference(hidden, norm_gain, w_query, w_key, w_value, w_out, kept_rows, kept_count):
    shards, capacity = kept_rows.shape
    per_shard = hidden.shape[0] // shards
    offsets = (jnp.arange(shards, dtype=jnp.int32) * per_shard)[:, None]
    positions = (offsets + kept_rows).reshape(-1).astype(jnp.int32)
    live_slot = (jnp.arange(capacity, dtype=jnp.int32)[None, :] < kept_count[:, None]).reshape(-1)
    gathered = hidden[positions]
    normed = rms_rows(gathered, norm_gain)
    slot_count = positions.shape[0]
    queries = jnp.dot(normed, w_query, preferred_element_type=jnp.float32).reshape(slot_count, Q_HEADS, HEAD_DIM)
    queries = rotary(queries, positions).astype(jnp.bfloat16)
    key_rows = jnp.dot(normed, w_key, preferred_element_type=jnp.float32).reshape(slot_count, KV_HEADS, HEAD_DIM)
    key_rows = rotary(key_rows, positions).astype(jnp.bfloat16)
    values = jnp.dot(normed, w_value, preferred_element_type=jnp.float32).astype(jnp.bfloat16)
    values = values.reshape(slot_count, KV_HEADS, HEAD_DIM)
    key_float = lax.optimization_barrier(key_rows).astype(jnp.float32)
    value_float = lax.optimization_barrier(values).astype(jnp.float32)
    query_float = lax.optimization_barrier(queries).astype(jnp.float32)
    query_float = query_float.reshape(shards, capacity, KV_HEADS, Q_HEADS // KV_HEADS, HEAD_DIM)
    query_pos = positions.reshape(shards, capacity)
    score_scale = 1.0 / math.sqrt(HEAD_DIM)

    def one_shard(operands):
        block_rows, block_pos = operands
        scores = jnp.einsum('rhgd,khd->rhgk', block_rows, key_float) * score_scale
        allowed = (live_slot[None, :] & (positions[None, :] <= block_pos[:, None]))[:, None, None, :]
        row_peak = lax.optimization_barrier(jnp.max(jnp.where(allowed, scores, -1e+30), axis=-1, keepdims=True))
        weights = jnp.where(allowed, jnp.exp(scores - row_peak), 0.0)
        row_total = lax.optimization_barrier(jnp.sum(weights, axis=-1))
        rounded = lax.optimization_barrier(weights.astype(jnp.bfloat16)).astype(jnp.float32)
        summed = jnp.einsum('rhgk,khd->rhgd', rounded, value_float)
        return (summed / row_total[..., None]).astype(jnp.bfloat16)
    attended = lax.map(one_shard, (query_float, query_pos)).reshape(slot_count, Q_HEADS * HEAD_DIM)
    projected = jnp.dot(attended, w_out, preferred_element_type=jnp.float32)
    updated = (gathered.astype(jnp.float32) + projected).astype(jnp.bfloat16)
    target = jnp.where(live_slot, positions, hidden.shape[0]).astype(jnp.int32)
    return hidden.at[target].set(updated, mode='drop')
```

```python
import functools
import math

import jax
import jax.numpy as jnp
from jax import lax
from jax.experimental import pallas as pl
from jax.experimental.pallas import tpu as pltpu
from jax.sharding import Mesh, PartitionSpec as P

WIDTH = 4096
Q_HEADS = 32
KV_HEADS = 4
HEAD_DIM = 128
EPSILON = 1e-05
ROPE_BASE = 10000.0
LOG2E = math.log2(math.e)
AXES = ("zh", "x", "y", "zl", "c")
SIZES = (2, 4, 4, 4, 2)
BF = jnp.bfloat16
F32 = jnp.float32
VMEM = pl.BlockSpec(memory_space=pltpu.VMEM)
SMEM = pl.BlockSpec(memory_space=pltpu.SMEM)
PARAMS = pltpu.CompilerParams(vmem_limit_bytes=48 * 2**20)


def hop(value, axis, step):
    size = SIZES[AXES.index(axis)]
    return lax.ppermute(value, axis, [(i, (i + step) % size) for i in range(size)])


def hop_mixed(value, first, step):
    pairs = []
    for x in range(4):
        for y in range(4):
            for c in range(2):
                if (c == 0) == first:
                    to = ((x + step) % 4, y)
                else:
                    to = (x, (y + step) % 4)
                pairs.append(((x * 4 + y) * 2 + c, (to[0] * 4 + to[1]) * 2 + c))
    return lax.ppermute(value, ("x", "y", "c"), pairs)


def ring_index(place):
    return lax.bitwise_and(place, 3)


def pick_body(coords, kept_ref, hidden_ref, out_ref):
    ctx = coords[0]
    wanted = kept_ref[pl.ds(ctx, 1), :]
    count = hidden_ref.shape[0]
    cap = wanted.shape[1]
    place = lax.broadcasted_iota(jnp.int32, (count, cap), 0)
    one_hot = (place == wanted).astype(F32).astype(BF)
    out_ref[...] = lax.dot_general(
        one_hot, hidden_ref[...], (((0,), (0,)), ((), ())), preferred_element_type=F32
    ).astype(BF)


def project_body(
    coords, f_ref, g_ref, gain_ref, cos_ref, sin_ref, t0, t1, t2, t3, q_ref, kv_ref, normed
):
    xi, yi, zi, core = coords[1], coords[2], coords[3], coords[4]
    cap = f_ref.shape[1]
    spread = jnp.zeros((cap, HEAD_DIM), F32)
    for ref in (f_ref, g_ref):
        for k in range(4):
            for b in range(4):
                v = ref[k, :, b * 128 : (b + 1) * 128].astype(F32)
                spread = spread + v * v
    scale = lax.rsqrt(jnp.sum(spread, axis=1, keepdims=True) * (1.0 / WIDTH) + EPSILON)
    for ref, side in ((f_ref, core), (g_ref, 1 - core)):
        for k in range(4):
            owner = ring_index(zi - k) * 2 + side
            half = lax.shift_right_logical(owner, 2)
            x = ring_index(owner)
            for y in range(4):
                v = ref[k, :, y * 128 : (y + 1) * 128].astype(F32)
                gain = gain_ref[:, pl.ds(pl.multiple_of(owner * 512 + y * 128, 128), 128)]
                block = jnp.where(core == 0, ring_index(yi - y), ring_index(xi - x))
                column = jnp.where(core == 0, x, y) * 256 + half * 128
                normed[block, :, pl.ds(pl.multiple_of(column, 128), 128)] = (
                    v * scale * gain
                ).astype(BF)
    total = jnp.dot(normed[0], t0[...], preferred_element_type=F32)
    for k, ref in ((1, t1), (2, t2), (3, t3)):
        total = total + jnp.dot(normed[k], ref[...], preferred_element_type=F32)
    cosine = cos_ref[...]
    sine = sin_ref[...]
    heads = q_ref.shape[1] // HEAD_DIM
    for h in range(heads + 1):
        v = total[:, h * HEAD_DIM : (h + 1) * HEAD_DIM]
        turned = pltpu.roll(v, HEAD_DIM // 2, 1)
        if h < heads:
            q_ref[:, h * HEAD_DIM : (h + 1) * HEAD_DIM] = (v * cosine + turned * sine).astype(BF)
        else:
            roped = (v * cosine + turned * sine).astype(BF)
            kv_ref[...] = jnp.where(core == 0, roped, v.astype(BF))


def attend_body(
    kb, coords, counts, q_ref, *refs
):
    k_refs, v_refs = refs[0:4], refs[4:8]
    out_ref, keys, vals, peak_ref, acc_ref = refs[8:]
    own, xi, yi = coords[0], coords[1], coords[2]
    cap, width = q_ref.shape
    heads = width // HEAD_DIM
    factor = LOG2E / math.sqrt(HEAD_DIM)

    row = lax.broadcasted_iota(jnp.int32, (cap, HEAD_DIM), 0)
    for k in range(4):
        for j in range(4):
            for half in range(2):
                at = (j * 2 + half) * cap
                shard = half * 16 + j * 4 + ring_index(yi - k)
                keys[pl.ds(pl.multiple_of(shard * cap, cap), cap), :] = k_refs[k][at : at + cap, :]
                shard = half * 16 + ring_index(xi - k) * 4 + j
                live = row < counts[shard]
                v = jnp.where(live, v_refs[k][at : at + cap, :].astype(F32), 0.0).astype(BF)
                spot = pl.ds(pl.multiple_of(shard * cap, cap), cap)
                vals[spot, :HEAD_DIM] = v
                vals[spot, HEAD_DIM:] = jnp.where(live, 1.0, 0.0).astype(BF)

    peak_ref[...] = jnp.full(peak_ref.shape, -1e30, F32)
    acc_ref[...] = jnp.zeros(acc_ref.shape, F32)
    first_own = own * cap

    def block(index, masked):
        start = pl.multiple_of(index * kb, kb)
        key_part = keys[pl.ds(start, kb), :]
        val_part = vals[pl.ds(start, kb), :]
        if masked:
            rows = lax.broadcasted_iota(jnp.int32, (cap, kb), 0)
            cols = lax.broadcasted_iota(jnp.int32, (cap, kb), 1)
            allowed = cols - rows <= first_own - start
        for h in range(heads):
            q = q_ref[:, h * HEAD_DIM : (h + 1) * HEAD_DIM]
            s = lax.dot_general(
                q, key_part, (((1,), (1,)), ((), ())), preferred_element_type=F32
            )
            if masked:
                s = jnp.where(allowed, s, -1e30)
            old = peak_ref[h]
            new = jnp.maximum(old, jnp.max(s, axis=1, keepdims=True))
            peak_ref[h] = new
            w = jnp.exp2((s - new[:, :1]) * factor).astype(BF)
            scale = jnp.exp2((old - new) * factor)
            acc_ref[h] = acc_ref[h] * jnp.concatenate([scale, scale], axis=1) + jnp.dot(
                w, val_part, preferred_element_type=F32
            )

    full = lax.div(first_own, kb)
    last = lax.div(first_own + (cap + kb - 1), kb)

    def plain(i, carry):
        block(i, False)
        return carry

    def edge(i, carry):
        block(i, True)
        return carry

    lax.fori_loop(0, full, plain, 0)
    lax.fori_loop(full, last, edge, 0)
    for h in range(heads):
        a = acc_ref[h]
        out_ref[:, h * HEAD_DIM : (h + 1) * HEAD_DIM] = (
            a[:, :HEAD_DIM] / a[:, HEAD_DIM:]
        ).astype(BF)


def out_body(coords, a_ref, w_ref, keep_ref, send_ref):
    zi, core = coords[3], coords[4]
    a = a_ref[...]
    for m in range(4):
        for mine in (True, False):
            owner = ring_index(zi + m) * 2 + (core if mine else 1 - core)
            half = lax.shift_right_logical(owner, 2)
            x = ring_index(owner)
            w = jnp.concatenate([w_ref[x, y, half] for y in range(4)], axis=1)
            part = jnp.dot(a, w, preferred_element_type=F32)
            if mine:
                keep_ref[m] = part
            else:
                send_ref[m] = part.astype(BF)


def place_body(coords, counts, kept_ref, hidden_ref, picked_ref, p0, p1, p2, p3, out_ref):
    ctx = coords[0]
    wanted = kept_ref[pl.ds(ctx, 1), :]
    count = hidden_ref.shape[0]
    cap = wanted.shape[1]
    projected = p0[...].astype(F32) + p1[...].astype(F32) + p2[...].astype(F32) + p3[...].astype(F32)
    updated = (picked_ref[...].astype(F32) + projected).astype(BF)
    place = lax.broadcasted_iota(jnp.int32, (count, cap), 0)
    slot = lax.broadcasted_iota(jnp.int32, (count, cap), 1)
    chosen = jnp.where((place == wanted) & (slot < counts[ctx]), 1.0, 0.0)
    replaced = jnp.sum(chosen, axis=1, keepdims=True) > 0.5
    moved = jnp.dot(chosen.astype(BF), updated, preferred_element_type=F32)
    out_ref[...] = jnp.where(replaced, moved, hidden_ref[...].astype(F32)).astype(BF)


def gather_xy(block):
    core = lax.axis_index("c")
    place = jnp.where(core == 0, lax.axis_index("x"), lax.axis_index("y"))
    got = [block] + [hop_mixed(block, True, k) for k in (1, 3, 2)]
    got = [got[0], got[1], got[3], got[2]]
    line = jnp.stack([got[0], got[3], got[2], got[1]] * 2)
    line = lax.dynamic_slice_in_dim(line, lax.rem(4 - place, 4), 4, 0)
    line = line.reshape((4 * block.shape[0],) + block.shape[1:])
    far = [hop_mixed(line, False, k) for k in (1, 3, 2)]
    return [line, far[0], far[2], far[1]]


def with_half(block):
    other = hop(block, "zh", 1)
    upper = lax.axis_index("zh") == 1
    return jnp.concatenate(
        [jnp.where(upper, other, block), jnp.where(upper, block, other)], axis=0
    )


def per_device(hidden, norm_gain, w_query, w_key, w_value, w_out, kept_rows, kept_count):
    cap = kept_rows.shape[1]
    heads = w_query.shape[1] // HEAD_DIM
    zh, x, y, zl, core = (lax.axis_index(a) for a in AXES)
    ctx = zh * 16 + x * 4 + y
    coords = jnp.stack([ctx, x, y, zl, core]).astype(jnp.int32)

    picked = pl.pallas_call(
        pick_body,
        out_shape=jax.ShapeDtypeStruct((cap, hidden.shape[1]), BF),
        in_specs=[SMEM, VMEM, VMEM],
        out_specs=VMEM,
    )(coords, kept_rows, hidden)

    w_kv = jnp.where(
        core == 0,
        lax.dynamic_slice_in_dim(w_key, zl * HEAD_DIM, HEAD_DIM, 1),
        lax.dynamic_slice_in_dim(w_value, zl * HEAD_DIM, HEAD_DIM, 1),
    )
    weights = gather_xy(with_half(jnp.concatenate([w_query, w_kv], axis=1)))

    pieces = jnp.stack([picked, hop(picked, "zl", 1), hop(picked, "zl", 2), hop(picked, "zl", 3)])
    others = hop(pieces, "c", 1)

    out_weights = lax.all_gather(w_out, "zh", axis=0)
    out_weights = lax.all_gather(out_weights, "y", axis=0)
    out_weights = lax.all_gather(out_weights, "x", axis=0)

    own_rows = lax.dynamic_index_in_dim(kept_rows, ctx, 0, keepdims=False)
    own_pos = ctx * hidden.shape[0] + own_rows
    exponent = jnp.arange(HEAD_DIM // 2, dtype=F32) * (2.0 / HEAD_DIM)
    inverse = jnp.exp(-math.log(ROPE_BASE) * exponent)
    angles = own_pos.astype(F32)[:, None] * inverse[None, :]
    cosine, sine = jnp.cos(angles), jnp.sin(angles)
    cosine = jnp.concatenate([cosine, cosine], axis=1)
    sine = jnp.concatenate([-sine, sine], axis=1)

    queries, own_kv = pl.pallas_call(
        project_body,
        out_shape=[
            jax.ShapeDtypeStruct((cap, heads * HEAD_DIM), BF),
            jax.ShapeDtypeStruct((cap, HEAD_DIM), BF),
        ],
        in_specs=[SMEM] + [VMEM] * 9,
        out_specs=[VMEM, VMEM],
        scratch_shapes=[pltpu.VMEM((4, cap, 1024), BF)],
        compiler_params=PARAMS,
    )(coords, pieces, others, norm_gain.reshape(1, -1), cosine, sine, *weights)

    mine = gather_xy(with_half(own_kv))
    theirs = [hop(part, "c", 1) for part in mine]
    key_parts = [jnp.where(core == 0, a, b) for a, b in zip(mine, theirs)]
    val_parts = [jnp.where(core == 0, b, a) for a, b in zip(mine, theirs)]

    slots = kept_rows.shape[0] * cap
    attended = pl.pallas_call(
        functools.partial(attend_body, 2048),
        out_shape=jax.ShapeDtypeStruct((cap, heads * HEAD_DIM), BF),
        in_specs=[SMEM, SMEM] + [VMEM] * 9,
        out_specs=VMEM,
        scratch_shapes=[
            pltpu.VMEM((slots, HEAD_DIM), BF),
            pltpu.VMEM((slots, 2 * HEAD_DIM), BF),
            pltpu.VMEM((heads, cap, HEAD_DIM), F32),
            pltpu.VMEM((heads, cap, 2 * HEAD_DIM), F32),
        ],
        compiler_params=PARAMS,
    )(coords, kept_count, queries, *key_parts, *val_parts)

    keep, send = pl.pallas_call(
        out_body,
        out_shape=[
            jax.ShapeDtypeStruct((4, cap, hidden.shape[1]), F32),
            jax.ShapeDtypeStruct((4, cap, hidden.shape[1]), BF),
        ],
        in_specs=[SMEM, VMEM, VMEM],
        out_specs=[VMEM, VMEM],
        compiler_params=PARAMS,
    )(coords, attended, out_weights)
    chip = (keep + hop(send, "c", 1).astype(F32)).astype(BF)
    parts = [chip[0]] + [hop(chip[m], "zl", m) for m in (1, 2, 3)]

    return pl.pallas_call(
        place_body,
        out_shape=jax.ShapeDtypeStruct(hidden.shape, BF),
        in_specs=[SMEM, SMEM] + [VMEM] * 7,
        out_specs=VMEM,
    )(coords, kept_count, kept_rows, hidden, picked, *parts)


def solution(mesh):
    ctx, tp = AXES[:3], AXES[3:]
    return jax.shard_map(
        per_device,
        mesh=Mesh(mesh.devices.reshape(SIZES), AXES),
        in_specs=(
            P(ctx, tp),
            P(),
            P(ctx, tp),
            P(ctx, None),
            P(ctx, None),
            P(tp, ctx),
            P(),
            P(),
        ),
        out_specs=P(ctx, tp),
        check_vma=False,
    )
```

```python
import functools
import math

import jax
import jax.numpy as jnp
from jax import lax
from jax.experimental import pallas as pl
from jax.experimental.pallas import tpu as pltpu
from jax.sharding import Mesh, PartitionSpec as P

WIDTH = 4096
Q_HEADS = 32
KV_HEADS = 4
HEAD_DIM = 128
EPSILON = 1e-05
ROPE_BASE = 10000.0
LOG2E = math.log2(math.e)
AXES = ("zh", "x", "y", "zl", "c")
SIZES = (2, 4, 4, 4, 2)
BF = jnp.bfloat16
F32 = jnp.float32
VMEM = pl.BlockSpec(memory_space=pltpu.VMEM)
ANY = pl.BlockSpec(memory_space=pl.ANY)
SMEM = pl.BlockSpec(memory_space=pltpu.SMEM)
PARAMS = pltpu.CompilerParams(vmem_limit_bytes=24 * 2**20)


def hop(value, axis, step):
    size = SIZES[AXES.index(axis)]
    return lax.ppermute(value, axis, [(i, (i + step) % size) for i in range(size)])


def hop_mixed(value, first, step):
    pairs = []
    for x in range(4):
        for y in range(4):
            for c in range(2):
                if (c == 0) == first:
                    to = ((x + step) % 4, y)
                else:
                    to = (x, (y + step) % 4)
                pairs.append(((x * 4 + y) * 2 + c, (to[0] * 4 + to[1]) * 2 + c))
    return lax.ppermute(value, ("x", "y", "c"), pairs)


def ring_index(place):
    return lax.bitwise_and(place, 3)


def pick_body(coords, kept_ref, hidden_ref, out_ref):
    ctx = coords[0]
    wanted = kept_ref[pl.ds(ctx, 1), :]
    count = hidden_ref.shape[0]
    cap = wanted.shape[1]
    place = lax.broadcasted_iota(jnp.int32, (count, cap), 0)
    one_hot = (place == wanted).astype(F32).astype(BF)
    out_ref[...] = lax.dot_general(
        one_hot, hidden_ref[...], (((0,), (0,)), ((), ())), preferred_element_type=F32
    ).astype(BF)


def tall(ref, at, first, last):
    return jnp.concatenate(
        [
            jnp.concatenate([ref[at, z, h * 128 : (h + 1) * 128, :] for h in range(first, last)], 1)
            for z in range(2)
        ],
        axis=0,
    )


def norm_body(
    heads, coords, counts, *refs
):
    xi, yi, zi, core = coords[1], coords[2], coords[3], coords[4]
    pieces = refs[0:8]
    gain_ref, cos_ref, sin_ref, t0, t1, t2a, t2b, t3, normed, kv_ref, held, sems = refs[8:]
    cap = held.shape[1]
    fetch([(piece, held.at[i]) for i, piece in enumerate(pieces)], sems)
    spread = jnp.zeros((cap, HEAD_DIM), F32)
    for i in range(8):
        for b in range(4):
            v = held[i, :, b * 128 : (b + 1) * 128].astype(F32)
            spread = spread + v * v
    scale = lax.rsqrt(jnp.sum(spread, axis=1, keepdims=True) * (1.0 / WIDTH) + EPSILON)
    for first, side in ((0, core), (4, 1 - core)):
        for k in range(4):
            owner = ring_index(zi - k) * 2 + side
            half = lax.shift_right_logical(owner, 2)
            x = ring_index(owner)
            for y in range(4):
                v = held[first + k, :, y * 128 : (y + 1) * 128].astype(F32)
                gain = gain_ref[:, pl.ds(pl.multiple_of(owner * 512 + y * 128, 128), 128)]
                block = jnp.where(core == 0, ring_index(yi - y), ring_index(xi - x))
                column = jnp.where(core == 0, x, y) * 256 + half * 128
                normed[block, :, pl.ds(pl.multiple_of(column, 128), 128)] = (
                    v * scale * gain
                ).astype(BF)
    total = jnp.zeros((cap, HEAD_DIM), F32)
    for k, j, ref, at in blocks_of((t0, t1, t2a, t2b, t3)):
        total = total + jnp.dot(
            normed[k, :, j * 256 : (j + 1) * 256],
            tall(ref, at, heads, heads + 1),
            preferred_element_type=F32,
        )
    turned = pltpu.roll(total, HEAD_DIM // 2, 1)
    roped = (total * cos_ref[...] + turned * sin_ref[...]).astype(BF)
    row = lax.broadcasted_iota(jnp.int32, total.shape, 0)
    value = jnp.where(row < counts[coords[0]], total, 0.0).astype(BF)
    kv_ref[...] = jnp.where(core == 0, roped, value)


def query_body(normed, cos_ref, sin_ref, t0, t1, t2a, t2b, t3, q_ref):
    heads = q_ref.shape[1] // HEAD_DIM
    total = jnp.zeros(q_ref.shape, F32)
    for k, j, ref, at in blocks_of((t0, t1, t2a, t2b, t3)):
        total = total + jnp.dot(
            normed[k, :, j * 256 : (j + 1) * 256],
            tall(ref, at, 0, heads),
            preferred_element_type=F32,
        )
    cosine = cos_ref[...]
    sine = sin_ref[...]
    for h in range(heads):
        v = total[:, h * HEAD_DIM : (h + 1) * HEAD_DIM]
        turned = pltpu.roll(v, HEAD_DIM // 2, 1)
        q_ref[:, h * HEAD_DIM : (h + 1) * HEAD_DIM] = (v * cosine + turned * sine).astype(BF)


def blocks_of(pieces):
    if len(pieces) == 4:
        for k, ref in enumerate(pieces):
            for j in range(4):
                yield k, j, ref, j
        return
    t0, t1, t2a, t2b, t3 = pieces
    for k, ref in ((0, t0), (1, t1), (3, t3)):
        for j in range(4):
            yield k, j, ref, j
    for j in range(4):
        yield 2, j, (t2a, t2b)[j // 2], j % 2


def arrange_body(cap, coords, counts, *refs):
    mine, theirs, (keys, vals, live) = refs[0:4], refs[4:8], refs[8:]
    xi, yi, core = coords[1], coords[2], coords[4]

    def fill(out, pieces, along_x):
        for k, j, ref, at in blocks_of(pieces):
            far = ring_index((yi if along_x else xi) - k)
            place = j * 4 + far if along_x else far * 4 + j
            for half in range(2):
                start = (at * 2 + half) * cap
                spot = pl.ds(pl.multiple_of((half * 16 + place) * cap, cap), cap)
                out[spot, :] = ref[start : start + cap, :]

    row = lax.broadcasted_iota(jnp.int32, (cap, HEAD_DIM), 0)
    for shard in range(live.shape[0] // cap):
        alive = jnp.where(row < counts[shard], 1.0, 0.0)
        live[shard * cap : (shard + 1) * cap, :] = alive.astype(BF)

    @pl.when(core == 0)
    def _():
        fill(keys, mine, True)
        fill(vals, theirs, False)

    @pl.when(core != 0)
    def _():
        fill(keys, theirs, True)
        fill(vals, mine, False)


def attend_body(kb, cap, first_row, coords, q_ref, keys, vals, live, out_ref, peak_ref, acc_ref):
    own = coords[0]
    rows, width = q_ref.shape
    heads = width // HEAD_DIM
    factor = LOG2E / math.sqrt(HEAD_DIM)
    peak_ref[...] = jnp.full(peak_ref.shape, -1e30, F32)
    acc_ref[...] = jnp.zeros(acc_ref.shape, F32)
    first_own = own * cap + first_row
    stacked = [
        jnp.concatenate(
            [q_ref[:, h * HEAD_DIM : (h + 1) * HEAD_DIM] for h in (g, g + 1)], axis=0
        )
        for g in range(0, heads, 2)
    ]

    def block(index, masked):
        start = pl.multiple_of(index * kb, kb)
        key_part = keys[pl.ds(start, kb), :]
        val_part = jnp.concatenate([vals[pl.ds(start, kb), :], live[pl.ds(start, kb), :]], axis=1)
        if masked:
            row = lax.broadcasted_iota(jnp.int32, (2 * rows, kb), 0)
            row = jnp.where(row >= rows, row - rows, row)
            col = lax.broadcasted_iota(jnp.int32, (2 * rows, kb), 1)
            allowed = col - row <= first_own - start
        scores = [
            lax.dot_general(q, key_part, (((1,), (1,)), ((), ())), preferred_element_type=F32)
            for q in stacked
        ]
        for g, s in enumerate(scores):
            if masked:
                s = jnp.where(allowed, s, -1e30)
            old = peak_ref[g]
            new = jnp.maximum(old, jnp.max(s, axis=1, keepdims=True))
            peak_ref[g] = new
            w = jnp.exp2((s - new[:, :1]) * factor).astype(BF)
            scale = jnp.exp2((old - new) * factor)
            acc_ref[g] = acc_ref[g] * jnp.concatenate([scale, scale], axis=1) + jnp.dot(
                w, val_part, preferred_element_type=F32
            )

    full = lax.div(first_own, kb)
    last = lax.div(first_own + (rows + kb - 1), kb)

    def plain(i, carry):
        block(i, False)
        return carry

    def edge(i, carry):
        block(i, True)
        return carry

    lax.fori_loop(0, full, plain, 0)
    lax.fori_loop(full, last, edge, 0)
    for g in range(heads // 2):
        a = acc_ref[g]
        done = (a[:, :HEAD_DIM] / a[:, HEAD_DIM:]).astype(BF)
        out_ref[:, 2 * g * HEAD_DIM : (2 * g + 1) * HEAD_DIM] = done[:rows]
        out_ref[:, (2 * g + 1) * HEAD_DIM : (2 * g + 2) * HEAD_DIM] = done[rows:]


def out_body(coords, a_ref, t0, t1, t2a, t2b, t3, keep_ref, send_ref, total):
    xi, yi, zi, core = coords[1], coords[2], coords[3], coords[4]
    a = a_ref[...]
    for k, j, ref, at in blocks_of((t0, t1, t2a, t2b, t3)):
        w = jnp.concatenate([ref[at, 0], ref[at, 1]], axis=1)
        part = jnp.dot(a, w, preferred_element_type=F32)
        x = jnp.where(core == 0, j, ring_index(xi - k))
        y = jnp.where(core == 0, ring_index(yi - k), j)
        for half in range(2):
            owner = half * 4 + x
            side = lax.bitwise_xor(lax.bitwise_and(owner, 1), core)
            turn = ring_index(lax.shift_right_logical(owner, 1) - zi)
            column = pl.ds(pl.multiple_of(y * 128, 128), 128)
            total[side * 4 + turn, :, column] = part[:, half * 128 : (half + 1) * 128]
    keep_ref[...] = total[0:4]
    send_ref[...] = total[4:8].astype(BF)


def place_body(coords, counts, kept_ref, hidden_ref, picked_ref, *refs):
    out_ref = refs[-1]
    ctx = coords[0]
    wanted = kept_ref[pl.ds(ctx, 1), :]
    count = hidden_ref.shape[0]
    cap = wanted.shape[1]
    sums = []
    for part in range(0, len(refs) - 1, 4):
        p0, p1, p2, p3 = (r[...].astype(F32) for r in refs[part : part + 4])
        sums.append(p0 + p1 + p2 + p3)
    projected = jnp.concatenate(sums, axis=0)
    updated = (picked_ref[...].astype(F32) + projected).astype(BF)
    place = lax.broadcasted_iota(jnp.int32, (count, cap), 0)
    slot = lax.broadcasted_iota(jnp.int32, (count, cap), 1)
    chosen = jnp.where((place == wanted) & (slot < counts[ctx]), 1.0, 0.0)
    replaced = jnp.sum(chosen, axis=1, keepdims=True) > 0.5
    moved = jnp.dot(chosen.astype(BF), updated, preferred_element_type=F32)
    out_ref[...] = jnp.where(replaced, moved, hidden_ref[...].astype(F32)).astype(BF)


def fetch(pairs, sems):
    copies = [pltpu.make_async_copy(a, b, sems.at[i]) for i, (a, b) in enumerate(pairs)]
    for copy in copies:
        copy.start()
    for copy in copies:
        copy.wait()


def pack_body(coords, q_any, k_any, v_any, o_any, out_ref, q_ref, k_ref, v_ref, o_ref, sems):
    fetch(((q_any, q_ref), (k_any, k_ref), (v_any, v_ref), (o_any, o_ref)), sems)
    zi, core = coords[3], coords[4]
    heads = q_ref.shape[1] // HEAD_DIM
    n = q_ref.shape[0]
    for h in range(heads):
        out_ref[h * n : (h + 1) * n, :] = q_ref[:, h * HEAD_DIM : (h + 1) * HEAD_DIM]
    own = pl.ds(pl.multiple_of(zi * HEAD_DIM, HEAD_DIM), HEAD_DIM)
    key = k_ref[:, own].astype(F32)
    val = v_ref[:, own].astype(F32)
    out_ref[heads * n : (heads + 1) * n, :] = jnp.where(core == 0, key, val).astype(BF)
    out_ref[(heads + 1) * n :, :] = o_ref[...]


def assemble_body(coords, *refs):
    parts, outs = refs[:8], refs[8:]
    place = jnp.where(coords[4] == 0, coords[1], coords[2])
    half = lax.shift_right_logical(coords[0], 4)
    for side in range(2):
        z = half if side == 0 else 1 - half
        for k in range(4):
            first = 0
            for out in outs:
                rows = out.shape[2]
                out[ring_index(place - k), z] = parts[side * 4 + k][first : first + rows, :]
                first += rows


def gather_near(coords, block, splits, *before_other):
    other = hop(block, "zh", 1)
    parts = [block] + [hop_mixed(block, True, k) for k in (1, 2, 3)]
    other = after(other, *before_other) if before_other else other
    parts += [other] + [hop_mixed(other, True, k) for k in (1, 2, 3)]
    return pl.pallas_call(
        assemble_body,
        out_shape=[jax.ShapeDtypeStruct((4, 2, n, block.shape[1]), BF) for n in splits],
        in_specs=[SMEM] + [VMEM] * 8,
        out_specs=[VMEM] * len(splits),
        compiler_params=PARAMS,
    )(coords, *parts)


def gather_far(line, *before_second):
    half = line.shape[0] // 2
    one, three = hop_mixed(line, False, 1), hop_mixed(line, False, 3)
    first, second = one[:half], three[half:]
    if before_second:
        first, second = after(first, *before_second), after(second, *before_second)
    two = hop_mixed(first, False, 1), hop_mixed(second, False, 3)
    return [line, one, two[0], two[1], three]


def cost(flops, exps=0):
    return pl.CostEstimate(flops=flops, bytes_accessed=4 * 2**20, transcendentals=exps)


def after(value, *earlier):
    return lax.optimization_barrier((value, *earlier))[0]


def per_device(hidden, norm_gain, w_query, w_key, w_value, w_out, kept_rows, kept_count):
    cap = kept_rows.shape[1]
    heads = w_query.shape[1] // HEAD_DIM
    zh, x, y, zl, core = (lax.axis_index(a) for a in AXES)
    ctx = zh * 16 + x * 4 + y
    coords = jnp.stack([ctx, x, y, zl, core]).astype(jnp.int32)

    q_rows = heads * HEAD_DIM
    block = pl.pallas_call(
        pack_body,
        out_shape=jax.ShapeDtypeStruct((q_rows + HEAD_DIM + w_out.shape[0], HEAD_DIM), BF),
        in_specs=[SMEM] + [ANY] * 4,
        out_specs=VMEM,
        scratch_shapes=[pltpu.VMEM(w.shape, BF) for w in (w_query, w_key, w_value, w_out)]
        + [pltpu.SemaphoreType.DMA((4,))],
        compiler_params=pltpu.CompilerParams(vmem_limit_bytes=56 * 2**20),
    )(coords, w_query, w_key, w_value, w_out)
    picked = pl.pallas_call(
        pick_body,
        out_shape=jax.ShapeDtypeStruct((cap, hidden.shape[1]), BF),
        in_specs=[SMEM, VMEM, VMEM],
        out_specs=VMEM,
    )(coords, kept_rows, hidden)
    near_in, near_out = gather_near(coords, block, (q_rows + HEAD_DIM, w_out.shape[0]), picked)
    one, three = hop(picked, "zl", 1), hop(picked, "zl", 3)
    near_in, one, three = lax.optimization_barrier((near_in, one, three))
    two = hop(after(picked, one, three), "zl", 2)
    in_weights = gather_far(near_in, two)
    two = after(two, in_weights[2], in_weights[3])
    out_weights = gather_far(after(near_out, in_weights[2], in_weights[3]))
    mine_rows = [picked, one, two, three]
    their_rows = [hop(part, "c", 1) for part in mine_rows]

    own_rows = lax.dynamic_index_in_dim(kept_rows, ctx, 0, keepdims=False)
    own_pos = ctx * hidden.shape[0] + own_rows
    exponent = jnp.arange(HEAD_DIM // 2, dtype=F32) * (2.0 / HEAD_DIM)
    inverse = jnp.exp(-math.log(ROPE_BASE) * exponent)
    angles = own_pos.astype(F32)[:, None] * inverse[None, :]
    cosine, sine = jnp.cos(angles), jnp.sin(angles)
    cosine = jnp.concatenate([cosine, cosine], axis=1)
    sine = jnp.concatenate([-sine, sine], axis=1)

    normed, own_kv = pl.pallas_call(
        functools.partial(norm_body, heads),
        out_shape=[
            jax.ShapeDtypeStruct((4, cap, 1024), BF),
            jax.ShapeDtypeStruct((cap, HEAD_DIM), BF),
        ],
        in_specs=[SMEM, SMEM] + [ANY] * 8 + [VMEM] * 8,
        out_specs=[VMEM, VMEM],
        scratch_shapes=[
            pltpu.VMEM((8, cap, hidden.shape[1]), BF),
            pltpu.SemaphoreType.DMA((8,)),
        ],
        compiler_params=PARAMS,
        cost_estimate=cost(2 * cap * WIDTH * HEAD_DIM * 4),
    )(coords, kept_count, *mine_rows, *their_rows, norm_gain.reshape(1, -1), cosine, sine, *in_weights)

    queries = pl.pallas_call(
        query_body,
        out_shape=jax.ShapeDtypeStruct((cap, q_rows), BF),
        in_specs=[VMEM] * 8,
        out_specs=VMEM,
        compiler_params=PARAMS,
        cost_estimate=cost(2 * cap * WIDTH * q_rows),
    )(normed, cosine, sine, *in_weights)

    (near_rows,) = gather_near(coords, own_kv, (cap,), queries, out_weights[1], out_weights[4])
    near_rows = near_rows.reshape(-1, HEAD_DIM)
    one, three, two = (hop_mixed(near_rows, False, k) for k in (1, 3, 2))
    mine = [near_rows, one, two, three]
    theirs = [hop(part, "c", 1) for part in mine]

    slots = kept_rows.shape[0] * cap
    keys, vals, live = pl.pallas_call(
        functools.partial(arrange_body, cap),
        out_shape=[
            jax.ShapeDtypeStruct((slots, HEAD_DIM), BF),
            jax.ShapeDtypeStruct((slots, HEAD_DIM), BF),
            jax.ShapeDtypeStruct((slots, HEAD_DIM), BF),
        ],
        in_specs=[SMEM, SMEM] + [VMEM] * 8,
        out_specs=[VMEM] * 3,
        compiler_params=PARAMS,
    )(coords, kept_count, *mine, *theirs)

    rows = cap // 2
    parts = []
    for first_row in (0, rows):
        attended = pl.pallas_call(
            functools.partial(attend_body, 2048, cap, first_row),
            out_shape=jax.ShapeDtypeStruct((rows, heads * HEAD_DIM), BF),
            in_specs=[SMEM] + [VMEM] * 4,
            out_specs=VMEM,
            scratch_shapes=[
                pltpu.VMEM((heads // 2, 2 * rows, HEAD_DIM), F32),
                pltpu.VMEM((heads // 2, 2 * rows, 2 * HEAD_DIM), F32),
            ],
            compiler_params=PARAMS,
            cost_estimate=cost(6 * rows * heads * HEAD_DIM * slots, rows * heads * slots),
        )(coords, after(queries[first_row : first_row + rows], *parts[:1]), keys, vals, live)
        keep, send = pl.pallas_call(
            out_body,
            out_shape=[
                jax.ShapeDtypeStruct((4, rows, hidden.shape[1]), F32),
                jax.ShapeDtypeStruct((4, rows, hidden.shape[1]), BF),
            ],
            in_specs=[SMEM] + [VMEM] * 6,
            out_specs=[VMEM, VMEM],
            scratch_shapes=[pltpu.VMEM((8, rows, hidden.shape[1]), F32)],
            compiler_params=PARAMS,
            cost_estimate=cost(2 * rows * heads * HEAD_DIM * WIDTH),
        )(coords, after(attended, *parts[1:]), *out_weights)
        got = hop(send, "c", 1)
        chip = [(keep[m] + got[m].astype(F32)).astype(BF) for m in range(4)]
        parts += [chip[0]] + [hop(chip[m], "zl", m) for m in (1, 2, 3)]

    return pl.pallas_call(
        place_body,
        out_shape=jax.ShapeDtypeStruct(hidden.shape, BF),
        in_specs=[SMEM, SMEM] + [VMEM] * 11,
        out_specs=VMEM,
    )(coords, kept_count, kept_rows, hidden, picked, *parts)


def solution(mesh):
    ctx, tp = AXES[:3], AXES[3:]
    return jax.shard_map(
        per_device,
        mesh=Mesh(mesh.devices.reshape(SIZES), AXES),
        in_specs=(
            P(ctx, tp),
            P(),
            P(ctx, tp),
            P(ctx, None),
            P(ctx, None),
            P(tp, ctx),
            P(),
            P(),
        ),
        out_specs=P(ctx, tp),
        check_vma=False,
    )
```

```python
import functools
import math

import jax
import jax.numpy as jnp
from jax import lax
from jax.experimental import pallas as pl
from jax.experimental.pallas import tpu as pltpu
from jax.sharding import Mesh, PartitionSpec as P

WIDTH = 4096
Q_HEADS = 32
KV_HEADS = 4
HEAD_DIM = 128
EPSILON = 1e-05
ROPE_BASE = 10000.0
LOG2E = math.log2(math.e)
AXES = ("zh", "x", "y", "zl", "c")
SIZES = (2, 4, 4, 4, 2)
BF = jnp.bfloat16
F32 = jnp.float32
VMEM = pl.BlockSpec(memory_space=pltpu.VMEM)
HBM = pl.BlockSpec(memory_space=pltpu.HBM)
SMEM = pl.BlockSpec(memory_space=pltpu.SMEM)
PARAMS = pltpu.CompilerParams(vmem_limit_bytes=12 * 2**20)
WIDE = pltpu.CompilerParams(vmem_limit_bytes=16 * 2**20)


def hop(value, axis, step):
    size = SIZES[AXES.index(axis)]
    return lax.ppermute(value, axis, [(i, (i + step) % size) for i in range(size)])


def hop_mixed(value, first, step):
    pairs = []
    for x in range(4):
        for y in range(4):
            for c in range(2):
                if (c == 0) == first:
                    to = ((x + step) % 4, y)
                else:
                    to = (x, (y + step) % 4)
                pairs.append(((x * 4 + y) * 2 + c, (to[0] * 4 + to[1]) * 2 + c))
    return lax.ppermute(value, ("x", "y", "c"), pairs)


def ring_index(place):
    return lax.bitwise_and(place, 3)


def pick_body(coords, kept_ref, hidden_ref, out_ref):
    ctx = coords[0]
    wanted = kept_ref[pl.ds(ctx, 1), :]
    count = hidden_ref.shape[0]
    cap = wanted.shape[1]
    place = lax.broadcasted_iota(jnp.int32, (count, cap), 0)
    one_hot = (place == wanted).astype(F32).astype(BF)
    out_ref[...] = lax.dot_general(
        one_hot, hidden_ref[...], (((0,), (0,)), ((), ())), preferred_element_type=F32
    ).astype(BF)


def tall(ref, at, first, last):
    return jnp.concatenate(
        [
            jnp.concatenate([ref[at, z, h * 128 : (h + 1) * 128, :] for h in range(first, last)], 1)
            for z in range(2)
        ],
        axis=0,
    )


def norm_body(
    coords, counts, *refs
):
    xi, yi, zi, core = coords[1], coords[2], coords[3], coords[4]
    m3, m1, o3, o1, gain_ref, cos_ref, sin_ref, t0, t1, t2, t3, normed, kv_ref = refs
    pieces = [m3.at[0], m3.at[1], m1, m3.at[2], o3.at[0], o3.at[1], o1, o3.at[2]]
    cap = pieces[0].shape[0]
    spread = jnp.zeros((cap, HEAD_DIM), F32)
    for i in range(8):
        for b in range(4):
            v = pieces[i][:, b * 128 : (b + 1) * 128].astype(F32)
            spread = spread + v * v
    scale = lax.rsqrt(jnp.sum(spread, axis=1, keepdims=True) * (1.0 / WIDTH) + EPSILON)
    for first, side in ((0, core), (4, 1 - core)):
        for k in range(4):
            owner = ring_index(zi - k) * 2 + side
            half = lax.shift_right_logical(owner, 2)
            x = ring_index(owner)
            for y in range(4):
                v = pieces[first + k][:, y * 128 : (y + 1) * 128].astype(F32)
                gain = gain_ref[:, pl.ds(pl.multiple_of(owner * 512 + y * 128, 128), 128)]
                block = jnp.where(core == 0, ring_index(yi - y), ring_index(xi - x))
                column = jnp.where(core == 0, x, y) * 256 + half * 128
                normed[block, :, pl.ds(pl.multiple_of(column, 128), 128)] = (
                    v * scale * gain
                ).astype(BF)
    total = jnp.zeros((cap, HEAD_DIM), F32)
    for k, j, ref, at in blocks_of((t0, t1, t2, t3)):
        total = total + jnp.dot(
            normed[k, :, j * 256 : (j + 1) * 256],
            tall(ref, at, 0, 1),
            preferred_element_type=F32,
        )
    turned = pltpu.roll(total, HEAD_DIM // 2, 1)
    roped = (total * cos_ref[...] + turned * sin_ref[...]).astype(BF)
    row = lax.broadcasted_iota(jnp.int32, total.shape, 0)
    value = jnp.where(row < counts[coords[0]], total, 0.0).astype(BF)
    kv_ref[...] = jnp.where(core == 0, roped, value)


def query_body(normed, cos_ref, sin_ref, t0, t1, t2a, t2b, t3, q_ref):
    heads = q_ref.shape[1] // HEAD_DIM
    total = jnp.zeros(q_ref.shape, F32)
    for k, j, ref, at in blocks_of((t0, t1, t2a, t2b, t3)):
        total = total + jnp.dot(
            normed[k, :, j * 256 : (j + 1) * 256],
            tall(ref, at, 0, heads),
            preferred_element_type=F32,
        )
    cosine = cos_ref[...]
    sine = sin_ref[...]
    for h in range(heads):
        v = total[:, h * HEAD_DIM : (h + 1) * HEAD_DIM]
        turned = pltpu.roll(v, HEAD_DIM // 2, 1)
        q_ref[:, h * HEAD_DIM : (h + 1) * HEAD_DIM] = (v * cosine + turned * sine).astype(BF)


def blocks_of(pieces):
    if len(pieces) == 4:
        for k, ref in enumerate(pieces):
            for j in range(4):
                yield k, j, ref, j
        return
    t0, t1, t2a, t2b, t3 = pieces
    for k, ref in ((0, t0), (1, t1), (3, t3)):
        for j in range(4):
            yield k, j, ref, j
    for j in range(4):
        yield 2, j, (t2a, t2b)[j // 2], j % 2


def arrange_body(cap, coords, counts, *refs):
    mine, theirs, (keys, vals, live) = refs[0:4], refs[4:8], refs[8:]
    xi, yi, core = coords[1], coords[2], coords[4]

    def fill(out, pieces, along_x):
        for k, j, ref, at in blocks_of(pieces):
            far = ring_index((yi if along_x else xi) - k)
            place = j * 4 + far if along_x else far * 4 + j
            for half in range(2):
                start = (at * 2 + half) * cap
                spot = pl.ds(pl.multiple_of((half * 16 + place) * cap, cap), cap)
                out[spot, :] = ref[start : start + cap, :]

    row = lax.broadcasted_iota(jnp.int32, (cap, HEAD_DIM), 0)
    for shard in range(live.shape[0] // cap):
        alive = jnp.where(row < counts[shard], 1.0, 0.0)
        live[shard * cap : (shard + 1) * cap, :] = alive.astype(BF)

    @pl.when(core == 0)
    def _():
        fill(keys, mine, True)
        fill(vals, theirs, False)

    @pl.when(core != 0)
    def _():
        fill(keys, theirs, True)
        fill(vals, mine, False)


def attend_body(kb, cap, first_row, coords, q_ref, keys, vals, live, out_ref, peak_ref, acc_ref):
    own = coords[0]
    rows, width = q_ref.shape
    heads = width // HEAD_DIM
    factor = LOG2E / math.sqrt(HEAD_DIM)
    peak_ref[...] = jnp.full(peak_ref.shape, -1e30, F32)
    acc_ref[...] = jnp.zeros(acc_ref.shape, F32)
    first_own = own * cap + first_row
    stacked = [
        jnp.concatenate(
            [q_ref[:, h * HEAD_DIM : (h + 1) * HEAD_DIM] for h in (g, g + 1)], axis=0
        )
        for g in range(0, heads, 2)
    ]

    def block(index, masked):
        start = pl.multiple_of(index * kb, kb)
        key_part = keys[pl.ds(start, kb), :]
        val_part = jnp.concatenate([vals[pl.ds(start, kb), :], live[pl.ds(start, kb), :]], axis=1)
        if masked:
            row = lax.broadcasted_iota(jnp.int32, (2 * rows, kb), 0)
            row = jnp.where(row >= rows, row - rows, row)
            col = lax.broadcasted_iota(jnp.int32, (2 * rows, kb), 1)
            allowed = col - row <= first_own - start
        scores = [
            lax.dot_general(q, key_part, (((1,), (1,)), ((), ())), preferred_element_type=F32)
            for q in stacked
        ]
        for g, s in enumerate(scores):
            if masked:
                s = jnp.where(allowed, s, -1e30)
            old = peak_ref[g]
            new = jnp.maximum(old, jnp.max(s, axis=1, keepdims=True))
            peak_ref[g] = new
            w = jnp.exp2((s - new[:, :1]) * factor).astype(BF)
            scale = jnp.exp2((old - new) * factor)
            acc_ref[g] = acc_ref[g] * jnp.concatenate([scale, scale], axis=1) + jnp.dot(
                w, val_part, preferred_element_type=F32
            )

    full = lax.div(first_own, kb)
    last = lax.div(first_own + (rows + kb - 1), kb)

    def plain(i, carry):
        block(i, False)
        return carry

    def edge(i, carry):
        block(i, True)
        return carry

    lax.fori_loop(0, full, plain, 0)
    lax.fori_loop(full, last, edge, 0)
    for g in range(heads // 2):
        a = acc_ref[g]
        done = (a[:, :HEAD_DIM] / a[:, HEAD_DIM:]).astype(BF)
        out_ref[:, 2 * g * HEAD_DIM : (2 * g + 1) * HEAD_DIM] = done[:rows]
        out_ref[:, (2 * g + 1) * HEAD_DIM : (2 * g + 2) * HEAD_DIM] = done[rows:]


def out_body(coords, a_ref, t0, t1, t2a, t2b, t3, keep_ref, send_ref, total):
    xi, yi, zi, core = coords[1], coords[2], coords[3], coords[4]
    a = a_ref[...]
    for k, j, ref, at in blocks_of((t0, t1, t2a, t2b, t3)):
        w = jnp.concatenate([ref[at, 0], ref[at, 1]], axis=1)
        part = jnp.dot(a, w, preferred_element_type=F32)
        x = jnp.where(core == 0, j, ring_index(xi - k))
        y = jnp.where(core == 0, ring_index(yi - k), j)
        for half in range(2):
            owner = half * 4 + x
            side = lax.bitwise_xor(lax.bitwise_and(owner, 1), core)
            turn = ring_index(lax.shift_right_logical(owner, 1) - zi)
            column = pl.ds(pl.multiple_of(y * 128, 128), 128)
            total[side * 4 + turn, :, column] = part[:, half * 128 : (half + 1) * 128]
    keep_ref[...] = total[0:4]
    send_ref[...] = total[4:8].astype(BF)


def place_body(coords, counts, kept_ref, hidden_ref, picked_ref, *refs):
    out_ref = refs[-1]
    ctx = coords[0]
    wanted = kept_ref[pl.ds(ctx, 1), :]
    count = hidden_ref.shape[0]
    cap = wanted.shape[1]
    sums = []
    for part in range(0, len(refs) - 1, 4):
        p0, p1, p2, p3 = (r[...].astype(F32) for r in refs[part : part + 4])
        sums.append(p0 + p1 + p2 + p3)
    projected = jnp.concatenate(sums, axis=0)
    updated = (picked_ref[...].astype(F32) + projected).astype(BF)
    place = lax.broadcasted_iota(jnp.int32, (count, cap), 0)
    slot = lax.broadcasted_iota(jnp.int32, (count, cap), 1)
    chosen = jnp.where((place == wanted) & (slot < counts[ctx]), 1.0, 0.0)
    replaced = jnp.sum(chosen, axis=1, keepdims=True) > 0.5
    moved = jnp.dot(chosen.astype(BF), updated, preferred_element_type=F32)
    out_ref[...] = jnp.where(replaced, moved, hidden_ref[...].astype(F32)).astype(BF)


def fetch(pairs, sems):
    copies = [pltpu.make_async_copy(a, b, sems.at[i]) for i, (a, b) in enumerate(pairs)]
    for copy in copies:
        copy.start()
    for copy in copies:
        copy.wait()


def pack_body(coords, q_any, k_any, v_any, o_any, out_ref, q_ref, k_ref, v_ref, o_ref, sems):
    fetch(((q_any, q_ref), (k_any, k_ref), (v_any, v_ref), (o_any, o_ref)), sems)
    zi, core = coords[3], coords[4]
    heads = q_ref.shape[1] // HEAD_DIM
    n = q_ref.shape[0]
    for h in range(heads):
        out_ref[h * n : (h + 1) * n, :] = q_ref[:, h * HEAD_DIM : (h + 1) * HEAD_DIM]
    own = pl.ds(pl.multiple_of(zi * HEAD_DIM, HEAD_DIM), HEAD_DIM)
    key = k_ref[:, own].astype(F32)
    val = v_ref[:, own].astype(F32)
    out_ref[heads * n : (heads + 1) * n, :] = jnp.where(core == 0, key, val).astype(BF)
    out_ref[(heads + 1) * n :, :] = o_ref[...]


def assemble_body(coords, *refs):
    parts, outs = refs[:8], refs[8:]
    place = jnp.where(coords[4] == 0, coords[1], coords[2])
    half = lax.shift_right_logical(coords[0], 4)
    for side in range(2):
        z = half if side == 0 else 1 - half
        for k in range(4):
            first = 0
            for out in outs:
                rows = out.shape[2]
                out[ring_index(place - k), z] = parts[side * 4 + k][first : first + rows, :]
                first += rows


def halves_body(coords, own_ref, other_ref, out_ref):
    half = lax.shift_right_logical(coords[0], 4)
    rows = own_ref.shape[0]
    out_ref[pl.ds(pl.multiple_of(half * rows, rows), rows), :] = own_ref[...]
    out_ref[pl.ds(pl.multiple_of((1 - half) * rows, rows), rows), :] = other_ref[...]


def line_body(coords, *refs):
    place = jnp.where(coords[4] == 0, coords[1], coords[2])
    for k in range(4):
        refs[4][ring_index(place - k)] = refs[k][...]


def gather_near(coords, block, other, splits):
    parts = [block] + [hop_mixed(block, True, k) for k in (1, 2, 3)]
    parts += [other] + [hop_mixed(other, True, k) for k in (1, 2, 3)]
    return pl.pallas_call(
        assemble_body,
        out_shape=[jax.ShapeDtypeStruct((4, 2, n, block.shape[1]), BF) for n in splits],
        in_specs=[SMEM] + [VMEM] * 8,
        out_specs=[VMEM] * len(splits),
        compiler_params=PARAMS,
    )(coords, *parts)


def gather_far(line, *before_second):
    half = line.shape[0] // 2
    one, three = hop_mixed(line, False, 1), hop_mixed(line, False, 3)
    first, second = one[:half], three[half:]
    if before_second:
        first, second = after(first, *before_second), after(second, *before_second)
    two = hop_mixed(first, False, 1), hop_mixed(second, False, 3)
    return [line, one, two[0], two[1], three]


def cost(flops, exps=0):
    return pl.CostEstimate(flops=flops, bytes_accessed=4 * 2**20, transcendentals=exps)


def after(value, *earlier):
    return lax.optimization_barrier((value, *earlier))[0]


def per_device(hidden, norm_gain, w_query, w_key, w_value, w_out, kept_rows, kept_count):
    cap = kept_rows.shape[1]
    heads = w_query.shape[1] // HEAD_DIM
    zh, x, y, zl, core = (lax.axis_index(a) for a in AXES)
    ctx = zh * 16 + x * 4 + y
    coords = jnp.stack([ctx, x, y, zl, core]).astype(jnp.int32)

    q_rows = heads * HEAD_DIM
    block = pl.pallas_call(
        pack_body,
        out_shape=jax.ShapeDtypeStruct((q_rows + HEAD_DIM + w_out.shape[0], HEAD_DIM), BF),
        in_specs=[SMEM] + [HBM] * 4,
        out_specs=VMEM,
        scratch_shapes=[pltpu.VMEM(w.shape, BF) for w in (w_query, w_key, w_value, w_out)]
        + [pltpu.SemaphoreType.DMA((4,))],
        compiler_params=PARAMS,
    )(coords, w_query, w_key, w_value, w_out)
    picked = pl.pallas_call(
        pick_body,
        out_shape=jax.ShapeDtypeStruct((cap, hidden.shape[1]), BF),
        in_specs=[SMEM, VMEM, VMEM],
        out_specs=VMEM,
    )(coords, kept_rows, hidden)
    other, picked = lax.optimization_barrier((hop(block, "zh", 1), picked))
    one, three = hop(picked, "zl", 1), hop(picked, "zl", 3)
    near_q, near_kv, near_out = gather_near(
        coords, block, other, (q_rows, HEAD_DIM, w_out.shape[0])
    )
    near_q, near_kv, one, three = lax.optimization_barrier((near_q, near_kv, one, three))
    two = hop(after(picked, one, three), "zl", 2)
    far = [hop_mixed(near_kv, False, k) for k in (1, 3, 2)]
    kv_weights = [near_kv, far[0], far[2], far[1]]
    mine3 = jnp.stack([picked, one, three])
    theirs3 = hop(mine3, "c", 1)
    q_weights = gather_far(after(near_q, *far, two, theirs3))
    near_out = after(near_out, q_weights[1], q_weights[4])
    out_one, out_three = hop_mixed(near_out, False, 1), hop_mixed(near_out, False, 3)
    theirs1 = hop(two, "c", 1)

    own_rows = lax.dynamic_index_in_dim(kept_rows, ctx, 0, keepdims=False)
    own_pos = ctx * hidden.shape[0] + own_rows
    exponent = jnp.arange(HEAD_DIM // 2, dtype=F32) * (2.0 / HEAD_DIM)
    inverse = jnp.exp(-math.log(ROPE_BASE) * exponent)
    angles = own_pos.astype(F32)[:, None] * inverse[None, :]
    cosine, sine = jnp.cos(angles), jnp.sin(angles)
    cosine = jnp.concatenate([cosine, cosine], axis=1)
    sine = jnp.concatenate([-sine, sine], axis=1)

    normed, own_kv = pl.pallas_call(
        norm_body,
        out_shape=[
            jax.ShapeDtypeStruct((4, cap, 1024), BF),
            jax.ShapeDtypeStruct((cap, HEAD_DIM), BF),
        ],
        in_specs=[SMEM, SMEM] + [VMEM] * 11,
        out_specs=[VMEM, VMEM],
        compiler_params=PARAMS,
        cost_estimate=cost(2 * cap * WIDTH * HEAD_DIM * 4),
    )(coords, kept_count, mine3, two, theirs3, theirs1, norm_gain.reshape(1, -1), cosine, sine, *kv_weights)

    queries = pl.pallas_call(
        query_body,
        out_shape=jax.ShapeDtypeStruct((cap, q_rows), BF),
        in_specs=[VMEM] * 8,
        out_specs=VMEM,
        compiler_params=PARAMS,
        cost_estimate=cost(2 * cap * WIDTH * q_rows),
    )(normed, cosine, sine, *q_weights)

    other_kv = hop(own_kv, "zh", 1)
    both_kv = pl.pallas_call(
        halves_body,
        out_shape=jax.ShapeDtypeStruct((2 * cap, HEAD_DIM), BF),
        in_specs=[SMEM, VMEM, VMEM],
        out_specs=VMEM,
    )(coords, own_kv, other_kv)
    both_kv = after(both_kv, q_weights[1], q_weights[4])
    line = [both_kv] + [hop_mixed(both_kv, True, k) for k in (1, 2, 3)]
    near_rows = pl.pallas_call(
        line_body,
        out_shape=jax.ShapeDtypeStruct((4, 2 * cap, HEAD_DIM), BF),
        in_specs=[SMEM] + [VMEM] * 4,
        out_specs=VMEM,
        compiler_params=PARAMS,
    )(coords, *line)
    near_rows = near_rows.reshape(-1, HEAD_DIM)
    one, three, two = (hop_mixed(near_rows, False, k) for k in (1, 3, 2))
    one, two, three, *_ = lax.optimization_barrier((one, two, three, queries, out_one, out_three))
    mine = [near_rows, one, two, three]
    theirs = [hop(part, "c", 1) for part in mine]

    slots = kept_rows.shape[0] * cap
    keys, vals, live = pl.pallas_call(
        functools.partial(arrange_body, cap),
        out_shape=[
            jax.ShapeDtypeStruct((slots, HEAD_DIM), BF),
            jax.ShapeDtypeStruct((slots, HEAD_DIM), BF),
            jax.ShapeDtypeStruct((slots, HEAD_DIM), BF),
        ],
        in_specs=[SMEM, SMEM] + [VMEM] * 8,
        out_specs=[VMEM] * 3,
        compiler_params=PARAMS,
    )(coords, kept_count, *mine, *theirs)

    half = near_out.shape[0] // 2
    out_weights = [
        near_out,
        out_one,
        hop_mixed(out_one[:half], False, 1),
        hop_mixed(out_three[half:], False, 3),
        out_three,
    ]
    rows = cap // 2
    parts = []
    for first_row in (0, rows):
        attended = pl.pallas_call(
            functools.partial(attend_body, 2048, cap, first_row),
            out_shape=jax.ShapeDtypeStruct((rows, heads * HEAD_DIM), BF),
            in_specs=[SMEM] + [VMEM] * 4,
            out_specs=VMEM,
            scratch_shapes=[
                pltpu.VMEM((heads // 2, 2 * rows, HEAD_DIM), F32),
                pltpu.VMEM((heads // 2, 2 * rows, 2 * HEAD_DIM), F32),
            ],
            compiler_params=WIDE,
            cost_estimate=cost(6 * rows * heads * HEAD_DIM * slots, rows * heads * slots),
        )(coords, after(queries[first_row : first_row + rows], *parts[:1]), keys, vals, live)
        keep, send = pl.pallas_call(
            out_body,
            out_shape=[
                jax.ShapeDtypeStruct((4, rows, hidden.shape[1]), F32),
                jax.ShapeDtypeStruct((4, rows, hidden.shape[1]), BF),
            ],
            in_specs=[SMEM] + [VMEM] * 6,
            out_specs=[VMEM, VMEM],
            scratch_shapes=[pltpu.VMEM((8, rows, hidden.shape[1]), F32)],
            compiler_params=PARAMS,
            cost_estimate=cost(2 * rows * heads * HEAD_DIM * WIDTH),
        )(coords, after(attended, *parts[1:]), *out_weights)
        got = hop(send, "c", 1)
        chip = [(keep[m] + got[m].astype(F32)).astype(BF) for m in range(4)]
        parts += [chip[0]] + [hop(chip[m], "zl", m) for m in (1, 2, 3)]

    return pl.pallas_call(
        place_body,
        out_shape=jax.ShapeDtypeStruct(hidden.shape, BF),
        in_specs=[SMEM, SMEM] + [VMEM] * 11,
        out_specs=VMEM,
    )(coords, kept_count, kept_rows, hidden, picked, *parts)


def solution(mesh):
    ctx, tp = AXES[:3], AXES[3:]
    return jax.shard_map(
        per_device,
        mesh=Mesh(mesh.devices.reshape(SIZES), AXES),
        in_specs=(
            P(ctx, tp),
            P(),
            P(ctx, tp),
            P(ctx, None),
            P(ctx, None),
            P(tp, ctx),
            P(),
            P(),
        ),
        out_specs=P(ctx, tp),
        check_vma=False,
    )
```

```python
import functools
import math

import jax
import jax.numpy as jnp
from jax import lax
from jax.experimental import pallas as pl
from jax.experimental.pallas import tpu as pltpu
from jax.sharding import Mesh, PartitionSpec as P

WIDTH = 4096
Q_HEADS = 32
KV_HEADS = 4
HEAD_DIM = 128
EPSILON = 1e-05
ROPE_BASE = 10000.0
LOG2E = math.log2(math.e)
AXES = ("zh", "x", "y", "zl", "c")
SIZES = (2, 4, 4, 4, 2)
BF = jnp.bfloat16
F32 = jnp.float32
VMEM = pl.BlockSpec(memory_space=pltpu.VMEM)
HBM = pl.BlockSpec(memory_space=pltpu.HBM)
SMEM = pl.BlockSpec(memory_space=pltpu.SMEM)
PARAMS = pltpu.CompilerParams(vmem_limit_bytes=12 * 2**20)
WIDE = pltpu.CompilerParams(vmem_limit_bytes=16 * 2**20)


def hop(value, axis, step):
    size = SIZES[AXES.index(axis)]
    return lax.ppermute(value, axis, [(i, (i + step) % size) for i in range(size)])


def hop_mixed(value, first, step):
    pairs = []
    for x in range(4):
        for y in range(4):
            for c in range(2):
                if (c == 0) == first:
                    to = ((x + step) % 4, y)
                else:
                    to = (x, (y + step) % 4)
                pairs.append(((x * 4 + y) * 2 + c, (to[0] * 4 + to[1]) * 2 + c))
    return lax.ppermute(value, ("x", "y", "c"), pairs)


def ring_index(place):
    return lax.bitwise_and(place, 3)


def pick_body(coords, kept_ref, hidden_ref, out_ref):
    ctx = coords[0]
    wanted = kept_ref[pl.ds(ctx, 1), :]
    count = hidden_ref.shape[0]
    cap = wanted.shape[1]
    place = lax.broadcasted_iota(jnp.int32, (count, cap), 0)
    one_hot = (place == wanted).astype(F32).astype(BF)
    out_ref[...] = lax.dot_general(
        one_hot, hidden_ref[...], (((0,), (0,)), ((), ())), preferred_element_type=F32
    ).astype(BF)


def tall(ref, at, first, last):
    return jnp.concatenate(
        [
            jnp.concatenate([ref[at, z, h * 128 : (h + 1) * 128, :] for h in range(first, last)], 1)
            for z in range(2)
        ],
        axis=0,
    )


def norm_body(
    coords, counts, *refs
):
    xi, yi, zi, core = coords[1], coords[2], coords[3], coords[4]
    m3, m1, o3, o1, gain_ref, cos_ref, sin_ref, t0, t1, t2, t3, normed, kv_ref = refs
    pieces = [m3.at[0], m3.at[1], m1, m3.at[2], o3.at[0], o3.at[1], o1, o3.at[2]]
    cap = pieces[0].shape[0]
    spread = jnp.zeros((cap, HEAD_DIM), F32)
    for i in range(8):
        for b in range(4):
            v = pieces[i][:, b * 128 : (b + 1) * 128].astype(F32)
            spread = spread + v * v
    scale = lax.rsqrt(jnp.sum(spread, axis=1, keepdims=True) * (1.0 / WIDTH) + EPSILON)
    for first, side in ((0, core), (4, 1 - core)):
        for k in range(4):
            owner = ring_index(zi - k) * 2 + side
            half = lax.shift_right_logical(owner, 2)
            x = ring_index(owner)
            for y in range(4):
                v = pieces[first + k][:, y * 128 : (y + 1) * 128].astype(F32)
                gain = gain_ref[:, pl.ds(pl.multiple_of(owner * 512 + y * 128, 128), 128)]
                block = jnp.where(core == 0, ring_index(yi - y), ring_index(xi - x))
                column = jnp.where(core == 0, x, y) * 256 + half * 128
                normed[block, :, pl.ds(pl.multiple_of(column, 128), 128)] = (
                    v * scale * gain
                ).astype(BF)
    total = jnp.zeros((cap, HEAD_DIM), F32)
    for k, j, ref, at in blocks_of((t0, t1, t2, t3)):
        total = total + jnp.dot(
            normed[k, :, j * 256 : (j + 1) * 256],
            tall(ref, at, 0, 1),
            preferred_element_type=F32,
        )
    turned = pltpu.roll(total, HEAD_DIM // 2, 1)
    roped = (total * cos_ref[...] + turned * sin_ref[...]).astype(BF)
    row = lax.broadcasted_iota(jnp.int32, total.shape, 0)
    value = jnp.where(row < counts[coords[0]], total, 0.0).astype(BF)
    kv_ref[...] = jnp.where(core == 0, roped, value)


def query_body(normed, cos_ref, sin_ref, t0, t1, t2a, t2b, t3, q_ref):
    heads = q_ref.shape[1] // HEAD_DIM
    total = jnp.zeros(q_ref.shape, F32)
    for k, j, ref, at in blocks_of((t0, t1, t2a, t2b, t3)):
        total = total + jnp.dot(
            normed[k, :, j * 256 : (j + 1) * 256],
            tall(ref, at, 0, heads),
            preferred_element_type=F32,
        )
    cosine = cos_ref[...]
    sine = sin_ref[...]
    for h in range(heads):
        v = total[:, h * HEAD_DIM : (h + 1) * HEAD_DIM]
        turned = pltpu.roll(v, HEAD_DIM // 2, 1)
        q_ref[:, h * HEAD_DIM : (h + 1) * HEAD_DIM] = (v * cosine + turned * sine).astype(BF)


def blocks_of(pieces):
    if len(pieces) == 4:
        for k, ref in enumerate(pieces):
            for j in range(4):
                yield k, j, ref, j
        return
    t0, t1, t2a, t2b, t3 = pieces
    for k, ref in ((0, t0), (1, t1), (3, t3)):
        for j in range(4):
            yield k, j, ref, j
    for j in range(4):
        yield 2, j, (t2a, t2b)[j // 2], j % 2


def arrange_body(cap, coords, counts, *refs):
    mine, theirs, (keys, vals, live) = refs[0:4], refs[4:8], refs[8:]
    xi, yi, core = coords[1], coords[2], coords[4]

    def fill(out, pieces, along_x):
        for k, j, ref, at in blocks_of(pieces):
            far = ring_index((yi if along_x else xi) - k)
            place = j * 4 + far if along_x else far * 4 + j
            for half in range(2):
                start = (at * 2 + half) * cap
                spot = pl.ds(pl.multiple_of((half * 16 + place) * cap, cap), cap)
                out[spot, :] = ref[start : start + cap, :]

    row = lax.broadcasted_iota(jnp.int32, (cap, HEAD_DIM), 0)
    for shard in range(live.shape[0] // cap):
        alive = jnp.where(row < counts[shard], 1.0, 0.0)
        live[shard * cap : (shard + 1) * cap, :] = alive.astype(BF)

    @pl.when(core == 0)
    def _():
        fill(keys, mine, True)
        fill(vals, theirs, False)

    @pl.when(core != 0)
    def _():
        fill(keys, theirs, True)
        fill(vals, mine, False)


def attend_body(kb, cap, first_row, coords, q_ref, keys, vals, live, out_ref, peak_ref, acc_ref):
    own = coords[0]
    rows, width = q_ref.shape
    heads = width // HEAD_DIM
    factor = LOG2E / math.sqrt(HEAD_DIM)
    peak_ref[...] = jnp.full(peak_ref.shape, -1e30, F32)
    acc_ref[...] = jnp.zeros(acc_ref.shape, F32)
    first_own = own * cap + first_row
    stacked = [
        jnp.concatenate(
            [q_ref[:, h * HEAD_DIM : (h + 1) * HEAD_DIM] for h in (g, g + 1)], axis=0
        )
        for g in range(0, heads, 2)
    ]

    def block(index, masked):
        start = pl.multiple_of(index * kb, kb)
        key_part = keys[pl.ds(start, kb), :]
        val_part = jnp.concatenate([vals[pl.ds(start, kb), :], live[pl.ds(start, kb), :]], axis=1)
        if masked:
            row = lax.broadcasted_iota(jnp.int32, (2 * rows, kb), 0)
            row = jnp.where(row >= rows, row - rows, row)
            col = lax.broadcasted_iota(jnp.int32, (2 * rows, kb), 1)
            allowed = col - row <= first_own - start
        scores = [
            lax.dot_general(q, key_part, (((1,), (1,)), ((), ())), preferred_element_type=F32)
            for q in stacked
        ]
        for g, s in enumerate(scores):
            if masked:
                s = jnp.where(allowed, s, -1e30)
            old = peak_ref[g]
            new = jnp.maximum(old, jnp.max(s, axis=1, keepdims=True))
            peak_ref[g] = new
            w = jnp.exp2((s - new[:, :1]) * factor).astype(BF)
            scale = jnp.exp2((old - new) * factor)
            acc_ref[g] = acc_ref[g] * jnp.concatenate([scale, scale], axis=1) + jnp.dot(
                w, val_part, preferred_element_type=F32
            )

    full = lax.div(first_own, kb)
    last = lax.div(first_own + (rows + kb - 1), kb)

    def plain(i, carry):
        block(i, False)
        return carry

    def edge(i, carry):
        block(i, True)
        return carry

    lax.fori_loop(0, full, plain, 0)
    lax.fori_loop(full, last, edge, 0)
    for g in range(heads // 2):
        a = acc_ref[g]
        done = (a[:, :HEAD_DIM] / a[:, HEAD_DIM:]).astype(BF)
        out_ref[:, 2 * g * HEAD_DIM : (2 * g + 1) * HEAD_DIM] = done[:rows]
        out_ref[:, (2 * g + 1) * HEAD_DIM : (2 * g + 2) * HEAD_DIM] = done[rows:]


def out_body(coords, a_ref, t0, t1, t2a, t2b, t3, keep_ref, send_ref, total):
    xi, yi, zi, core = coords[1], coords[2], coords[3], coords[4]
    a = a_ref[...]
    for k, j, ref, at in blocks_of((t0, t1, t2a, t2b, t3)):
        w = jnp.concatenate([ref[at, 0], ref[at, 1]], axis=1)
        part = jnp.dot(a, w, preferred_element_type=F32)
        x = jnp.where(core == 0, j, ring_index(xi - k))
        y = jnp.where(core == 0, ring_index(yi - k), j)
        for half in range(2):
            owner = half * 4 + x
            side = lax.bitwise_xor(lax.bitwise_and(owner, 1), core)
            turn = ring_index(lax.shift_right_logical(owner, 1) - zi)
            column = pl.ds(pl.multiple_of(y * 128, 128), 128)
            total[side * 4 + turn, :, column] = part[:, half * 128 : (half + 1) * 128]
    keep_ref[...] = total[0:4]
    send_ref[...] = total[4:8].astype(BF)


def place_body(coords, counts, kept_ref, hidden_ref, picked_ref, *refs):
    out_ref = refs[-1]
    ctx = coords[0]
    wanted = kept_ref[pl.ds(ctx, 1), :]
    count = hidden_ref.shape[0]
    cap = wanted.shape[1]
    sums = []
    for part in range(0, len(refs) - 1, 4):
        p0, p1, p2, p3 = (r[...].astype(F32) for r in refs[part : part + 4])
        sums.append(p0 + p1 + p2 + p3)
    projected = jnp.concatenate(sums, axis=0)
    updated = (picked_ref[...].astype(F32) + projected).astype(BF)
    place = lax.broadcasted_iota(jnp.int32, (count, cap), 0)
    slot = lax.broadcasted_iota(jnp.int32, (count, cap), 1)
    chosen = jnp.where((place == wanted) & (slot < counts[ctx]), 1.0, 0.0)
    replaced = jnp.sum(chosen, axis=1, keepdims=True) > 0.5
    moved = jnp.dot(chosen.astype(BF), updated, preferred_element_type=F32)
    out_ref[...] = jnp.where(replaced, moved, hidden_ref[...].astype(F32)).astype(BF)


def fetch(pairs, sems):
    copies = [pltpu.make_async_copy(a, b, sems.at[i]) for i, (a, b) in enumerate(pairs)]
    for copy in copies:
        copy.start()
    for copy in copies:
        copy.wait()


def pack_body(coords, q_any, k_any, v_any, o_any, out_ref, q_ref, k_ref, v_ref, o_ref, sems):
    fetch(((q_any, q_ref), (k_any, k_ref), (v_any, v_ref), (o_any, o_ref)), sems)
    zi, core = coords[3], coords[4]
    heads = q_ref.shape[1] // HEAD_DIM
    n = q_ref.shape[0]
    for h in range(heads):
        out_ref[h * n : (h + 1) * n, :] = q_ref[:, h * HEAD_DIM : (h + 1) * HEAD_DIM]
    own = pl.ds(pl.multiple_of(zi * HEAD_DIM, HEAD_DIM), HEAD_DIM)
    key = k_ref[:, own].astype(F32)
    val = v_ref[:, own].astype(F32)
    out_ref[heads * n : (heads + 1) * n, :] = jnp.where(core == 0, key, val).astype(BF)
    out_ref[(heads + 1) * n :, :] = o_ref[...]


def assemble_body(coords, *refs):
    parts, outs = refs[:8], refs[8:]
    place = jnp.where(coords[4] == 0, coords[1], coords[2])
    half = lax.shift_right_logical(coords[0], 4)
    for side in range(2):
        z = half if side == 0 else 1 - half
        for k in range(4):
            first = 0
            for out in outs:
                rows = out.shape[2]
                out[ring_index(place - k), z] = parts[side * 4 + k][first : first + rows, :]
                first += rows


def halves_body(coords, own_ref, other_ref, out_ref):
    half = lax.shift_right_logical(coords[0], 4)
    rows = own_ref.shape[0]
    out_ref[pl.ds(pl.multiple_of(half * rows, rows), rows), :] = own_ref[...]
    out_ref[pl.ds(pl.multiple_of((1 - half) * rows, rows), rows), :] = other_ref[...]


def line_body(coords, *refs):
    place = jnp.where(coords[4] == 0, coords[1], coords[2])
    for k in range(4):
        refs[4][ring_index(place - k)] = refs[k][...]


def gather_near(coords, block, other, splits):
    parts = [block] + [hop_mixed(block, True, k) for k in (1, 2, 3)]
    parts += [other] + [hop_mixed(other, True, k) for k in (1, 2, 3)]
    return pl.pallas_call(
        assemble_body,
        out_shape=[jax.ShapeDtypeStruct((4, 2, n, block.shape[1]), BF) for n in splits],
        in_specs=[SMEM] + [VMEM] * 8,
        out_specs=[VMEM] * len(splits),
        compiler_params=PARAMS,
    )(coords, *parts)


def gather_far(line, *before_second):
    half = line.shape[0] // 2
    one, three = hop_mixed(line, False, 1), hop_mixed(line, False, 3)
    first, second = one[:half], three[half:]
    if before_second:
        first, second = after(first, *before_second), after(second, *before_second)
    two = hop_mixed(first, False, 1), hop_mixed(second, False, 3)
    return [line, one, two[0], two[1], three]


def cost(flops, exps=0):
    return pl.CostEstimate(flops=flops, bytes_accessed=4 * 2**20, transcendentals=exps)


def after(value, *earlier):
    return lax.optimization_barrier((value, *earlier))[0]


def per_device(hidden, norm_gain, w_query, w_key, w_value, w_out, kept_rows, kept_count):
    cap = kept_rows.shape[1]
    heads = w_query.shape[1] // HEAD_DIM
    zh, x, y, zl, core = (lax.axis_index(a) for a in AXES)
    ctx = zh * 16 + x * 4 + y
    coords = jnp.stack([ctx, x, y, zl, core]).astype(jnp.int32)

    q_rows = heads * HEAD_DIM
    block = pl.pallas_call(
        pack_body,
        out_shape=jax.ShapeDtypeStruct((q_rows + HEAD_DIM + w_out.shape[0], HEAD_DIM), BF),
        in_specs=[SMEM] + [HBM] * 4,
        out_specs=VMEM,
        scratch_shapes=[pltpu.VMEM(w.shape, BF) for w in (w_query, w_key, w_value, w_out)]
        + [pltpu.SemaphoreType.DMA((4,))],
        compiler_params=PARAMS,
    )(coords, w_query, w_key, w_value, w_out)
    picked = pl.pallas_call(
        pick_body,
        out_shape=jax.ShapeDtypeStruct((cap, hidden.shape[1]), BF),
        in_specs=[SMEM, VMEM, VMEM],
        out_specs=VMEM,
    )(coords, kept_rows, hidden)
    other, picked = lax.optimization_barrier((hop(block, "zh", 1), picked))
    one, three = hop(picked, "zl", 1), hop(picked, "zl", 3)
    near_q, near_kv, near_out = gather_near(
        coords, block, other, (q_rows, HEAD_DIM, w_out.shape[0])
    )
    near_q, near_kv, one, three = lax.optimization_barrier((near_q, near_kv, one, three))
    two = hop(after(picked, one, three), "zl", 2)
    far = [hop_mixed(near_kv, False, k) for k in (1, 3, 2)]
    kv_weights = [near_kv, far[0], far[2], far[1]]
    mine3 = jnp.stack([picked, one, three])
    theirs3 = hop(mine3, "c", 1)
    q_weights = gather_far(after(near_q, *far, two))
    near_out = after(near_out, q_weights[1], q_weights[4])
    out_one, out_three = hop_mixed(near_out, False, 1), hop_mixed(near_out, False, 3)
    theirs1 = hop(two, "c", 1)

    own_rows = lax.dynamic_index_in_dim(kept_rows, ctx, 0, keepdims=False)
    own_pos = ctx * hidden.shape[0] + own_rows
    exponent = jnp.arange(HEAD_DIM // 2, dtype=F32) * (2.0 / HEAD_DIM)
    inverse = jnp.exp(-math.log(ROPE_BASE) * exponent)
    angles = own_pos.astype(F32)[:, None] * inverse[None, :]
    cosine, sine = jnp.cos(angles), jnp.sin(angles)
    cosine = jnp.concatenate([cosine, cosine], axis=1)
    sine = jnp.concatenate([-sine, sine], axis=1)

    normed, own_kv = pl.pallas_call(
        norm_body,
        out_shape=[
            jax.ShapeDtypeStruct((4, cap, 1024), BF),
            jax.ShapeDtypeStruct((cap, HEAD_DIM), BF),
        ],
        in_specs=[SMEM, SMEM] + [VMEM] * 11,
        out_specs=[VMEM, VMEM],
        compiler_params=PARAMS,
        cost_estimate=cost(2 * cap * WIDTH * HEAD_DIM * 4),
    )(coords, kept_count, mine3, two, theirs3, theirs1, norm_gain.reshape(1, -1), cosine, sine, *kv_weights)

    queries = pl.pallas_call(
        query_body,
        out_shape=jax.ShapeDtypeStruct((cap, q_rows), BF),
        in_specs=[VMEM] * 8,
        out_specs=VMEM,
        compiler_params=PARAMS,
        cost_estimate=cost(2 * cap * WIDTH * q_rows),
    )(normed, cosine, sine, *q_weights)

    other_kv = hop(own_kv, "zh", 1)
    both_kv = pl.pallas_call(
        halves_body,
        out_shape=jax.ShapeDtypeStruct((2 * cap, HEAD_DIM), BF),
        in_specs=[SMEM, VMEM, VMEM],
        out_specs=VMEM,
    )(coords, own_kv, other_kv)
    both_kv = after(both_kv, q_weights[1], q_weights[4])
    line = [both_kv] + [hop_mixed(both_kv, True, k) for k in (1, 2, 3)]
    near_rows = pl.pallas_call(
        line_body,
        out_shape=jax.ShapeDtypeStruct((4, 2 * cap, HEAD_DIM), BF),
        in_specs=[SMEM] + [VMEM] * 4,
        out_specs=VMEM,
        compiler_params=PARAMS,
    )(coords, *line)
    near_rows = near_rows.reshape(-1, HEAD_DIM)
    one, three, two = (hop_mixed(near_rows, False, k) for k in (1, 3, 2))
    one, two, three, *_ = lax.optimization_barrier((one, two, three, queries, out_one, out_three))
    mine = [near_rows, one, two, three]
    theirs = [hop(part, "c", 1) for part in mine]

    slots = kept_rows.shape[0] * cap
    keys, vals, live = pl.pallas_call(
        functools.partial(arrange_body, cap),
        out_shape=[
            jax.ShapeDtypeStruct((slots, HEAD_DIM), BF),
            jax.ShapeDtypeStruct((slots, HEAD_DIM), BF),
            jax.ShapeDtypeStruct((slots, HEAD_DIM), BF),
        ],
        in_specs=[SMEM, SMEM] + [VMEM] * 8,
        out_specs=[VMEM] * 3,
        compiler_params=PARAMS,
    )(coords, kept_count, *mine, *theirs)

    half = near_out.shape[0] // 2
    out_weights = [
        near_out,
        out_one,
        hop_mixed(out_one[:half], False, 1),
        hop_mixed(out_three[half:], False, 3),
        out_three,
    ]
    rows = cap // 2
    parts = []
    for first_row in (0, rows):
        attended = pl.pallas_call(
            functools.partial(attend_body, 2048, cap, first_row),
            out_shape=jax.ShapeDtypeStruct((rows, heads * HEAD_DIM), BF),
            in_specs=[SMEM] + [VMEM] * 4,
            out_specs=VMEM,
            scratch_shapes=[
                pltpu.VMEM((heads // 2, 2 * rows, HEAD_DIM), F32),
                pltpu.VMEM((heads // 2, 2 * rows, 2 * HEAD_DIM), F32),
            ],
            compiler_params=WIDE,
            cost_estimate=cost(6 * rows * heads * HEAD_DIM * slots, rows * heads * slots),
        )(coords, after(queries[first_row : first_row + rows], *parts[:1]), keys, vals, live)
        keep, send = pl.pallas_call(
            out_body,
            out_shape=[
                jax.ShapeDtypeStruct((4, rows, hidden.shape[1]), F32),
                jax.ShapeDtypeStruct((4, rows, hidden.shape[1]), BF),
            ],
            in_specs=[SMEM] + [VMEM] * 6,
            out_specs=[VMEM, VMEM],
            scratch_shapes=[pltpu.VMEM((8, rows, hidden.shape[1]), F32)],
            compiler_params=PARAMS,
            cost_estimate=cost(2 * rows * heads * HEAD_DIM * WIDTH),
        )(coords, after(attended, *parts[1:]), *out_weights)
        got = hop(send, "c", 1)
        chip = [(keep[m] + got[m].astype(F32)).astype(BF) for m in range(4)]
        parts += [chip[0]] + [hop(chip[m], "zl", m) for m in (1, 2, 3)]

    return pl.pallas_call(
        place_body,
        out_shape=jax.ShapeDtypeStruct(hidden.shape, BF),
        in_specs=[SMEM, SMEM] + [VMEM] * 11,
        out_specs=VMEM,
    )(coords, kept_count, kept_rows, hidden, picked, *parts)


def solution(mesh):
    ctx, tp = AXES[:3], AXES[3:]
    return jax.shard_map(
        per_device,
        mesh=Mesh(mesh.devices.reshape(SIZES), AXES),
        in_specs=(
            P(ctx, tp),
            P(),
            P(ctx, tp),
            P(ctx, None),
            P(ctx, None),
            P(tp, ctx),
            P(),
            P(),
        ),
        out_specs=P(ctx, tp),
        check_vma=False,
    )
```
